128 devices in a mesh: node: 8 (over z_lo, x), local: 16 (over y, z_hi, core).
Axes of the slice: x: 4, y: 4, z: 4 (z_hi: 2, z_lo: 2; z = z_hi * 2 + z_lo), core: 2. Of those that a mesh axis runs over, the one named last changes fastest.
Arguments:
- tokens: bfloat16 [131072, 8192], P(('node', 'local')), may hold values from -24 to 24
- positions: int32 [131072], P(('node', 'local')), may hold values from 0 to 4095
- weight_codes: bfloat16 [8192, 512], P('local'), may hold values from -4 to 4
- weight_scales: float32 [8192, 2], P('local'), may hold values from 0.00390625 to 0.03125
- key_cotangent: bfloat16 [131072, 512], P(('node', 'local')), may hold values from -6 to 6
Outputs:
- keys: bfloat16 [131072, 512], P(('node', 'local'))
- weight_grad: float32 [8192, 512], P(('node', 'local'))
The draws below stay inside these ranges and needn't reach their ends.
All inputs are finite; a program needn't handle non-finite values.
Results may differ from the reference program's by a relative error of at most 0.0029.
Values may be sent and summed in bfloat16 or wider, within the bound.
No kernel may reach another device: no remote copies, remote signals or barrier semaphores. Data moves between devices by JAX's collectives and lax.ppermute only.
A program may use at most 128 MiB of HBM per device.

```python
import jax
import jax.numpy as jnp

D = 8192
HD = 128
BLOCK = 256
HK = 512
TOKENS = 131072


def draw_weight_scales(key, part):
    key = jax.random.fold_in(key, 7)
    exponent = jax.random.randint(key, (D, HK // BLOCK), -8, -4)
    return jnp.exp2(exponent.astype(jnp.float32))


def with_ends(array, stream_key, low, top_value):
    longest = array.shape.index(max(array.shape))
    spots = []
    for shift in (0, 1):
        where = [jax.random.randint(jax.random.fold_in(stream_key, axis), (), 0, length) for axis, length in enumerate(array.shape)]
        where[longest] = (where[longest] + shift) % array.shape[longest]
        spots.append(tuple(where))
    return array.at[spots[0]].set(low).at[spots[1]].set(top_value)


def raised(result, rng, source, target, blocks, factor):
    owner, partner = [(jnp.arange(result.shape[dim]) // (result.shape[dim] // blocks)).reshape([-1 if axis == dim else 1 for axis in range(result.ndim)]) for dim in (source, target)]
    chosen = jax.random.permutation(rng, blocks)[partner]
    strong = (owner == chosen) | (owner == (partner + blocks // 2) % blocks)
    return jnp.where(strong, factor * result, result)


def levels(stream_key, dims, cuts, low, high):
    def one(dim, blocks):
        steps = jax.random.uniform(jax.random.fold_in(jax.random.fold_in(stream_key, 6), dim), (blocks,), jnp.float32, low / len(cuts), high / len(cuts))
        return jnp.repeat(jnp.exp(steps), dims[dim] // blocks).reshape((-1,) + (1,) * (len(dims) - dim - 1))

    level = one(*cuts[0])
    for cut in cuts[1:]:
        level = level * one(*cut)
    return level


def centred(stream_key, shape, spread, reach, shards=(), kind=jnp.bfloat16):
    array = spread * jax.random.normal(stream_key, shape, jnp.float32)
    if shards:
        array = array * levels(stream_key, shape, shards, -0.22, 0.18)
    return jnp.clip(array, -reach, reach).astype(kind)


def gaussian_with(stream_key, dims, spread, limit, shards, heavy, held_as=jnp.bfloat16):
    entries = spread * jax.random.normal(stream_key, dims, jnp.float32)
    if shards:
        entries = entries * levels(stream_key, dims, shards, -0.22, 0.18)
    return jnp.clip(raised(entries, jax.random.fold_in(stream_key, 3), *heavy), -limit, limit).astype(held_as)


def setup_inputs(seed: int = 0) -> dict:
    key_list = jax.random.split(jax.random.key(seed), 6)
    return {
        "tokens": gaussian_with(key_list[0], (TOKENS, D), 1.0, 24.0, ((0, 128),), (0, 1, 128, 5.5)),
        "positions": with_ends(jax.random.randint(key_list[1], (TOKENS,), 0, 4096), jax.random.fold_in(key_list[1], 1), 0, 4095).astype(jnp.int32),
        "weight_codes": centred(key_list[2], (D, HK), 1.0, 4.0, ((0, 16),)),
        "weight_scales": draw_weight_scales(jax.random.fold_in(key_list[5], 71), 0),
        "key_cotangent": centred(key_list[4], (TOKENS, HK), 1.0, 6.0, ((0, 128),)),
    }


def rotation(positions, head):
    half = head // 2
    freq = 10000.0 ** (-(2.0 * jnp.arange(half, dtype=jnp.float32)) / head)
    angle = positions.astype(jnp.float32)[:, None] * freq[None, :]
    return jnp.cos(angle)[:, None, :], jnp.sin(angle)[:, None, :]


def reference(tokens, positions, weight_codes, weight_scales, key_cotangent):
    rows = tokens.shape[0]
    heads = HK // HD
    half = HD // 2
    weight = (weight_codes.astype(jnp.float32) * jnp.repeat(weight_scales, BLOCK, axis=1)).astype(jnp.bfloat16)
    raw = jnp.dot(tokens, weight, preferred_element_type=jnp.float32).reshape(rows, heads, HD)
    cosine, sine = rotation(positions, HD)
    first, second = raw[..., :half], raw[..., half:]
    keys = jnp.concatenate([first * cosine - second * sine, second * cosine + first * sine], axis=-1)
    keys = keys.reshape(rows, HK).astype(jnp.bfloat16)
    grads = key_cotangent.astype(jnp.float32).reshape(rows, heads, HD)
    gfirst, gsecond = grads[..., :half], grads[..., half:]
    back = jnp.concatenate([gfirst * cosine + gsecond * sine, gsecond * cosine - gfirst * sine], axis=-1)
    back = back.reshape(rows, HK).astype(jnp.bfloat16)
    weight_grad = jnp.dot(tokens.T, back, preferred_element_type=jnp.float32)
    return keys, weight_grad
```

```python
import jax
import jax.numpy as jnp
from jax import lax
from jax.experimental import pallas as pl
from jax.experimental.pallas import tpu as pltpu
from jax.sharding import Mesh, PartitionSpec as P

HD = 128
HALF = 64
BLOCK = 256
BF16 = jnp.bfloat16
F32 = jnp.float32
MIB = 1024 * 1024
BITS = ("zlo", "xhi", "xlo", "yhi", "ylo", "zhi", "core")
LIMIT = 8 * MIB
LARGE = 36 * MIB
VMEM = pl.BlockSpec(memory_space=pltpu.VMEM)
SCALAR = pl.BlockSpec(memory_space=pltpu.SMEM)
NEAR, BACK = (1, 3), (3, 1)


def coordinates(device):
    return (device >> 4) & 3, (device >> 2) & 3, device >> 6, (device >> 1) & 1, device & 1


def side(v, core):
    return v & 1 if core else v >> 1


def quads():
    groups = {}
    for device in range(128):
        x, y, zlo, zhi, core = coordinates(device)
        sides = side(x, core), side(y, core)
        name = core, *(v ^ BACK[core] * s for v, s in zip((x, y), sides))
        groups.setdefault(name, []).append((zlo, *sides, zhi, device))
    return [[member[-1] for member in sorted(members)] for members in groups.values()]


STAY = (0, 0)


def send(value, x=STAY, y=STAY, z=STAY, core=STAY):
    pairs = []
    for src in range(128):
        at_x, at_y, zlo, zhi, at_core = coordinates(src)
        at_z = (2 * zhi + zlo) ^ z[at_core]
        place = ((at_z & 1) << 6) | ((at_x ^ x[at_core]) << 4) | ((at_y ^ y[at_core]) << 2) | ((at_z >> 1) << 1)
        pairs.append((src, place | (at_core ^ core[at_core])))
    return lax.ppermute(value, BITS, pairs)


def held_at(distance, core):
    near = jnp.where(core == 0, 1, 3)
    return jnp.where(distance == 0, 0, jnp.where(distance == 2, 3, jnp.where(distance == near, 1, 2)))


def weight_kernel(at, codes_ref, scales_ref, piece_ref, scaled):
    scales = jnp.concatenate([scales_ref[...]] * 4, axis=0).T
    for block in range(2):
        columns = slice(block * BLOCK, (block + 1) * BLOCK)
        scaled[:, columns] = (codes_ref[:, columns].astype(F32) * scales[:, block : block + 1]).astype(BF16)
    piece_ref[0] = scaled[pl.ds(pl.multiple_of(at[2] * 256, 256), 256)]


def weight_piece(at, codes, scales):
    rows, width = codes.shape
    return pl.pallas_call(
        weight_kernel,
        in_specs=[SCALAR, VMEM, VMEM],
        out_specs=VMEM,
        out_shape=jax.ShapeDtypeStruct((1, rows // 2, width), BF16),
        scratch_shapes=[pltpu.VMEM((rows, width), BF16)],
        compiler_params=pltpu.CompilerParams(vmem_limit_bytes=LIMIT),
        name="weight",
    )(at, codes, scales)


def back_kernel(cotangent_ref, cos_ref, sin_ref, back_ref, cos2_ref, sin2_ref):
    cos = jnp.concatenate([cos_ref[...], cos_ref[...]], axis=0).T
    sin = jnp.concatenate([-sin_ref[...], sin_ref[...]], axis=0).T
    cos2_ref[...] = cos
    sin2_ref[...] = sin
    for head in range(4):
        given = cotangent_ref[:, head * HD : (head + 1) * HD].astype(F32)
        back_ref[:, head * HD : (head + 1) * HD] = (given * cos - pltpu.roll(given, HALF, 1) * sin).astype(BF16)


def back_of(cotangent, cos, sin):
    rows, width = cotangent.shape
    turn = jax.ShapeDtypeStruct((rows, HD), F32)
    return pl.pallas_call(
        back_kernel,
        in_specs=[VMEM] * 3,
        out_specs=[VMEM] * 3,
        out_shape=[jax.ShapeDtypeStruct((rows, width), BF16), turn, turn],
        compiler_params=pltpu.CompilerParams(vmem_limit_bytes=LIMIT),
        name="back",
    )(cotangent, cos, sin)


def grad_kernel(chunk, at, back_ref, tokens_ref, own_ref, sib_ref, kept_ref, arrived):
    x, y, zlo, core = at[0], at[1], at[2], at[4]

    def fetch(i):
        column = pl.multiple_of(((zlo ^ chunk) * 4 + i) * 1024, 1024)
        return pltpu.make_async_copy(tokens_ref.at[:, pl.ds(column, 1024)], kept_ref.at[i], arrived.at[i])

    def place(to, here, holder):
        low, high = (to ^ here) & 1, (to ^ here) >> 1
        return jnp.where(holder == 0, to >> 1, to & 1), high ^ (low & (1 - holder))

    for i in range(4):
        fetch(i).start()
    for i in range(4):
        fetch(i).wait()
        for pair in range(2):
            block = kept_ref[i, :, pair * 512 : (pair + 1) * 512]
            part = lax.dot_general(block, back_ref[...], (((0,), (0,)), ((), ())), preferred_element_type=F32)
            for j in range(4):
                to_y, to_zhi = 2 * pair + j // 2, j % 2
                halves = part[j * 128 : j * 128 + 64], part[j * 128 + 64 : (j + 1) * 128]
                for ref, holder, half in (
                    (own_ref, core, jnp.where(core == 0, halves[0], halves[1])),
                    (sib_ref, 1 - core, jnp.where(core == 0, halves[1], halves[0])),
                ):
                    ref[(*place(i, x, holder), *place(to_y, y, holder), to_zhi)] = half.astype(ref.dtype)


def grad_half(at, back, tokens, chunk):
    rows, width = back.shape
    blocks = (2, 2, 2, 2, 2, 64, width)
    return pl.pallas_call(
        lambda *refs: grad_kernel(chunk, *refs),
        in_specs=[SCALAR, VMEM, pl.BlockSpec(memory_space=pltpu.HBM)],
        out_specs=[VMEM, VMEM],
        out_shape=[
            jax.ShapeDtypeStruct(blocks, F32),
            jax.ShapeDtypeStruct(blocks, BF16),
        ],
        scratch_shapes=[pltpu.VMEM((4, rows, 1024), BF16), pltpu.SemaphoreType.DMA((4,))],
        compiler_params=pltpu.CompilerParams(vmem_limit_bytes=LARGE),
        cost_estimate=pl.CostEstimate(flops=20 * rows * 4096 * width, bytes_accessed=8 * MIB, transcendentals=0),
        name="grad",
    )(at, back, tokens)


def forward_kernel(other, at, tokens_ref, weight_ref, *rest):
    y, zlo, zhi, core = at[1], at[2], at[3], at[4]
    acc, weight, block, arrived, filled = rest[-5:]
    holder = core ^ other

    def fetch(i):
        column = pl.multiple_of((2 * i + holder) * 512, 512)
        return pltpu.make_async_copy(tokens_ref.at[:, pl.ds(column, 512)], block.at[i], arrived.at[i])

    def fill(i, to_zlo):
        from_y = held_at(y ^ (i // 2), holder)
        from_z = held_at((2 * zhi + zlo) ^ (2 * (i % 2) + to_zlo), holder)
        rows = pl.ds(to_zlo * 256, 256)
        return pltpu.make_async_copy(
            weight_ref.at[from_z * 4 + from_y], weight.at[i, rows], filled.at[2 * i + to_zlo]
        )

    for i in range(8):
        fetch(i).start()
        fill(i, 0).start()
        fill(i, 1).start()
    acc[...] = rest[0][...] if other else jnp.zeros_like(acc)

    @pl.loop(0, 8)
    def _(i):
        fetch(i).wait()
        fill(i, 0).wait()
        fill(i, 1).wait()
        acc[...] += jnp.dot(block[i], weight[i], preferred_element_type=F32)

    if other:
        cos_ref, sin_ref, keys_ref = rest[1:4]
        for head in range(4):
            raw = acc[:, head * HD : (head + 1) * HD]
            turned = pltpu.roll(raw, HALF, 1)
            keys_ref[:, head * HD : (head + 1) * HD] = (raw * cos_ref[...] + turned * sin_ref[...]).astype(BF16)


def forward(at, tokens, weight, *rest):
    rows, depth = tokens.shape
    width = weight.shape[-1]
    hbm = pl.BlockSpec(memory_space=pltpu.HBM)
    total = pltpu.VMEM((rows, width), F32)
    return pl.pallas_call(
        lambda *refs: forward_kernel(int(bool(rest)), *refs),
        in_specs=[SCALAR, hbm, hbm] + [VMEM] * len(rest),
        out_specs=VMEM,
        scratch_shapes=[total] * bool(rest)
        + [
            pltpu.VMEM((8, 512, width), BF16),
            pltpu.VMEM((8, rows, 512), BF16),
            pltpu.SemaphoreType.DMA((8,)),
            pltpu.SemaphoreType.DMA((16,)),
        ],
        out_shape=jax.ShapeDtypeStruct((rows, width), BF16 if rest else F32),
        compiler_params=pltpu.CompilerParams(vmem_limit_bytes=LARGE),
        cost_estimate=pl.CostEstimate(flops=4 * rows * depth * width, bytes_accessed=4 * MIB, transcendentals=0),
        name="forward",
    )(at, tokens, weight, *rest)


def sums_kernel(at, near_ref, near_in_ref, far_ref, far_in_ref, out_ref):
    zlo = at[2]
    for kx in range(2):
        for ky in range(2):
            out_ref[zlo, kx, ky] = (near_ref[kx, 0, ky] + near_in_ref[kx, ky].astype(F32)).astype(BF16)
            out_ref[1 - zlo, kx, ky] = (far_ref[kx, ky, 0] + far_in_ref[kx, ky].astype(F32)).astype(BF16)


def sums(at, near, near_in, far, far_in):
    out = (2, *near_in.shape)
    return pl.pallas_call(
        sums_kernel,
        in_specs=[SCALAR] + [VMEM] * 4,
        out_specs=VMEM,
        out_shape=jax.ShapeDtypeStruct(out, BF16),
        compiler_params=pltpu.CompilerParams(vmem_limit_bytes=LIMIT),
        name="sums",
    )(at, near, near_in, far, far_in)


def local(tokens, positions, weight_codes, weight_scales, key_cotangent):
    x, y, zlo, zhi, core = coordinates(lax.axis_index(BITS))
    at = jnp.stack([x, y, zlo, zhi, core]).astype(jnp.int32)
    tie = lax.optimization_barrier

    weight = weight_piece(at, weight_codes, weight_scales.T)
    weight_got = send(weight, y=NEAR)

    freq = 10000.0 ** (-(2.0 * jnp.arange(HALF, dtype=F32)) / HD)
    angle = freq[:, None] * positions.astype(F32)[None, :]
    cos, sin = jnp.cos(angle), jnp.sin(angle)
    back, cos, sin = back_of(key_cotangent, cos, sin)

    weight = jnp.concatenate([weight, weight_got])
    back, weight = tie((back, weight))
    weight_got = send(weight, y=BACK)

    far, far_sib = grad_half(at, back, tokens, 1)
    far_got = send(far_sib, core=(1, 1))
    weight = jnp.concatenate([weight, weight_got])
    far, back, weight = tie((far, back, weight))
    weight_got = send(weight[:2], z=NEAR)
    near, near_sib = grad_half(at, back, tokens, 0)
    near, near_sib, far_got, weight_got = tie((near, near_sib, far_got, weight_got))
    near_got = send(near_sib, core=(1, 1))
    weight_more = send(weight[2:], z=NEAR)

    def total(own, got, ax, ay):
        return own[:, ax, :, ay] + got[:, ax, :, ay].astype(F32)

    both = slice(None)
    far_in = send(total(far, far_got, 1, both).astype(BF16), x=NEAR)
    near_in = send(total(near, near_got, both, 1).astype(BF16), y=NEAR)
    weight = jnp.concatenate([weight, weight_got, weight_more])
    weight_got = send(weight, z=BACK)
    far_sent = (total(far, far_got, 0, 1) + far_in[:, :, 1].astype(F32)).astype(BF16)
    near_sent = (total(near, near_got, 1, 0) + near_in[:, 1].astype(F32)).astype(BF16)
    far = total(far, far_got, 0, both) + far_in.astype(F32)
    near = total(near, near_got, both, 0) + near_in.astype(F32)
    far_in = send(far_sent, y=NEAR)
    near_in = send(near_sent, x=NEAR)
    mine = sums(at, near, near_in, far, far_in).reshape(16, 64, 512)
    got = lax.all_to_all(mine, BITS, 0, 0, axis_index_groups=quads(), tiled=True)
    at, weight_got, _ = tie((at, weight_got, mine))
    weight = jnp.concatenate([weight, weight_got])
    weight_sib = send(weight, core=(1, 1))
    half = forward(at, tokens, weight)
    keys = forward(at, tokens, weight_sib, half, cos, sin)
    keys, got = tie((keys, got))
    return keys, jnp.sum(got.astype(F32), axis=0)


def solution(mesh):
    bits = Mesh(mesh.devices.reshape((2,) * 7), BITS)
    tokens, weight = P(BITS, None), P(("yhi", "ylo", "zhi", "core"), None)
    return jax.shard_map(
        local,
        mesh=bits,
        in_specs=(tokens, P(BITS), weight, weight, tokens),
        out_specs=(tokens, tokens),
        check_vma=False,
    )
```

```python
import jax
import jax.numpy as jnp
from jax import lax
from jax.experimental import pallas as pl
from jax.experimental.pallas import tpu as pltpu
from jax.sharding import Mesh, PartitionSpec as P

HD = 128
HALF = 64
BLOCK = 256
BF16 = jnp.bfloat16
F32 = jnp.float32
MIB = 1024 * 1024
BITS = ("zlo", "xhi", "xlo", "yhi", "ylo", "zhi", "core")
LIMIT = 8 * MIB
LARGE = 36 * MIB
COVER = 4
VMEM = pl.BlockSpec(memory_space=pltpu.VMEM)
SCALAR = pl.BlockSpec(memory_space=pltpu.SMEM)
NEAR, BACK = (1, 3), (3, 1)


def coordinates(device):
    return (device >> 4) & 3, (device >> 2) & 3, device >> 6, (device >> 1) & 1, device & 1


def side(v, core):
    return v & 1 if core else v >> 1


def quads():
    groups = {}
    for device in range(128):
        x, y, zlo, zhi, core = coordinates(device)
        sides = side(x, core), side(y, core)
        name = core, *(v ^ BACK[core] * s for v, s in zip((x, y), sides))
        groups.setdefault(name, []).append((zlo, *sides, zhi, device))
    return [[member[-1] for member in sorted(members)] for members in groups.values()]


STAY = (0, 0)


def send(what, value, x=STAY, y=STAY, z=STAY, core=STAY):
    pairs = []
    for src in range(128):
        at_x, at_y, zlo, zhi, at_core = coordinates(src)
        at_z = (2 * zhi + zlo) ^ z[at_core]
        place = ((at_z & 1) << 6) | ((at_x ^ x[at_core]) << 4) | ((at_y ^ y[at_core]) << 2) | ((at_z >> 1) << 1)
        pairs.append((src, place | (at_core ^ core[at_core])))
    with jax.named_scope(what):
        return lax.ppermute(value, BITS, pairs)


def held_at(distance, core):
    near = jnp.where(core == 0, 1, 3)
    return jnp.where(distance == 0, 0, jnp.where(distance == 2, 3, jnp.where(distance == near, 1, 2)))


def weight_kernel(at, codes_ref, scales_ref, piece_ref, scaled):
    scales = jnp.concatenate([scales_ref[...]] * 4, axis=0).T
    for block in range(2):
        columns = slice(block * BLOCK, (block + 1) * BLOCK)
        scaled[:, columns] = (codes_ref[:, columns].astype(F32) * scales[:, block : block + 1]).astype(BF16)
    piece_ref[0] = scaled[pl.ds(pl.multiple_of(at[2] * 256, 256), 256)]


def weight_piece(at, codes, scales):
    rows, width = codes.shape
    return pl.pallas_call(
        weight_kernel,
        in_specs=[SCALAR, VMEM, VMEM],
        out_specs=VMEM,
        out_shape=jax.ShapeDtypeStruct((1, rows // 2, width), BF16),
        scratch_shapes=[pltpu.VMEM((rows, width), BF16)],
        compiler_params=pltpu.CompilerParams(vmem_limit_bytes=LIMIT),
        name="weight",
    )(at, codes, scales)


def head_turn(cos_ref, sin_ref):
    cos, sin = cos_ref[...], sin_ref[...]
    return jnp.concatenate([cos, cos], axis=0).T, jnp.concatenate([-sin, sin], axis=0).T


def back_kernel(cotangent_ref, cos_ref, sin_ref, back_ref):
    cos, sin = head_turn(cos_ref, sin_ref)
    for head in range(4):
        given = cotangent_ref[:, head * HD : (head + 1) * HD].astype(F32)
        back_ref[:, head * HD : (head + 1) * HD] = (given * cos - pltpu.roll(given, HALF, 1) * sin).astype(BF16)


def back_of(cotangent, cos, sin):
    return pl.pallas_call(
        back_kernel,
        in_specs=[VMEM] * 3,
        out_specs=VMEM,
        out_shape=jax.ShapeDtypeStruct(cotangent.shape, BF16),
        compiler_params=pltpu.CompilerParams(vmem_limit_bytes=LIMIT),
        name="back",
    )(cotangent, cos, sin)


def grad_kernel(chunk, at, back_ref, tokens_ref, own_ref, sib_ref, kept_ref, arrived):
    x, y, zlo, core = at[0], at[1], at[2], at[4]

    def fetch(i):
        column = pl.multiple_of(((zlo ^ chunk) * 4 + i) * 1024, 1024)
        return pltpu.make_async_copy(tokens_ref.at[:, pl.ds(column, 1024)], kept_ref.at[i], arrived.at[i])

    def place(to, here, holder):
        low, high = (to ^ here) & 1, (to ^ here) >> 1
        return jnp.where(holder == 0, to >> 1, to & 1), high ^ (low & (1 - holder))

    for i in range(4):
        fetch(i).start()
    for i in range(4):
        fetch(i).wait()
        for pair in range(2):
            block = kept_ref[i, :, pair * 512 : (pair + 1) * 512]
            part = lax.dot_general(block, back_ref[...], (((0,), (0,)), ((), ())), preferred_element_type=F32)
            for j in range(4):
                to_y, to_zhi = 2 * pair + j // 2, j % 2
                halves = part[j * 128 : j * 128 + 64], part[j * 128 + 64 : (j + 1) * 128]
                for ref, holder, half in (
                    (own_ref, core, jnp.where(core == 0, halves[0], halves[1])),
                    (sib_ref, 1 - core, jnp.where(core == 0, halves[1], halves[0])),
                ):
                    ref[(*place(i, x, holder), *place(to_y, y, holder), to_zhi)] = half.astype(ref.dtype)


def grad_half(at, back, tokens, chunk):
    rows, width = back.shape
    blocks = (2, 2, 2, 2, 2, 64, width)
    return pl.pallas_call(
        lambda *refs: grad_kernel(chunk, *refs),
        in_specs=[SCALAR, VMEM, pl.BlockSpec(memory_space=pltpu.HBM)],
        out_specs=[VMEM, VMEM],
        out_shape=[
            jax.ShapeDtypeStruct(blocks, F32),
            jax.ShapeDtypeStruct(blocks, BF16),
        ],
        scratch_shapes=[pltpu.VMEM((4, rows, 1024), BF16), pltpu.SemaphoreType.DMA((4,))],
        compiler_params=pltpu.CompilerParams(vmem_limit_bytes=LARGE),
        cost_estimate=pl.CostEstimate(flops=20 * rows * 4096 * width, bytes_accessed=8 * MIB, transcendentals=0),
        name="grad",
    )(at, back, tokens)


def forward_kernel(other, at, tokens_ref, *rest):
    y, zlo, zhi, core = at[1], at[2], at[3], at[4]
    parts, rest = rest[:4], rest[4:]
    acc, weight, block, arrived, filled = rest[-5:]
    holder = core ^ other

    def fetch(i):
        column = pl.multiple_of((2 * i + holder) * 512, 512)
        return pltpu.make_async_copy(tokens_ref.at[:, pl.ds(column, 512)], block.at[i], arrived.at[i])

    def fill(i, to_zlo, ref, place):
        rows = pl.ds(to_zlo * 256, 256)
        return pltpu.make_async_copy(ref.at[place], weight.at[i, rows], filled.at[2 * i + to_zlo])

    def start_fill(i, to_zlo):
        from_y = held_at(y ^ (i // 2), holder)
        from_z = held_at((2 * zhi + zlo) ^ (2 * (i % 2) + to_zlo), holder)
        for n, ref in enumerate(parts):

            @pl.when((from_z // 2) * 2 + from_y // 2 == n)
            def _():
                fill(i, to_zlo, ref, (from_z % 2) * 2 + from_y % 2).start()

    for i in range(8):
        fetch(i).start()
        start_fill(i, 0)
        start_fill(i, 1)
    acc[...] = rest[0][...] if other else jnp.zeros_like(acc)

    @pl.loop(0, 8)
    def _(i):
        fetch(i).wait()
        fill(i, 0, parts[0], 0).wait()
        fill(i, 1, parts[0], 0).wait()
        acc[...] += jnp.dot(block[i], weight[i], preferred_element_type=F32)

    if other:
        cos, sin = head_turn(*rest[1:3])
        keys_ref = rest[3]
        for head in range(4):
            raw = acc[:, head * HD : (head + 1) * HD]
            turned = pltpu.roll(raw, HALF, 1)
            keys_ref[:, head * HD : (head + 1) * HD] = (raw * cos + turned * sin).astype(BF16)


def forward(at, tokens, parts, *rest):
    rows, depth = tokens.shape
    width = parts[0].shape[-1]
    hbm = pl.BlockSpec(memory_space=pltpu.HBM)
    total = pltpu.VMEM((rows, width), F32)
    return pl.pallas_call(
        lambda *refs: forward_kernel(int(bool(rest)), *refs),
        in_specs=[SCALAR] + [hbm] * 5 + [VMEM] * len(rest),
        out_specs=VMEM,
        scratch_shapes=[total] * bool(rest)
        + [
            pltpu.VMEM((8, 512, width), BF16),
            pltpu.VMEM((8, rows, 512), BF16),
            pltpu.SemaphoreType.DMA((8,)),
            pltpu.SemaphoreType.DMA((16,)),
        ],
        out_shape=jax.ShapeDtypeStruct((rows, width), BF16 if rest else F32),
        compiler_params=pltpu.CompilerParams(vmem_limit_bytes=LARGE),
        cost_estimate=pl.CostEstimate(flops=COVER * rows * depth * width, bytes_accessed=4 * MIB, transcendentals=0),
        name="forward",
    )(at, tokens, *parts, *rest)


def total_kernel(got_ref, out_ref, block, arrived):
    def fetch(i):
        return pltpu.make_async_copy(got_ref.at[4 * i : 4 * i + 4], block.at[i], arrived.at[i])

    for i in range(4):
        fetch(i).start()
    for i in range(4):
        fetch(i).wait()
        part = jnp.sum(block[i].astype(F32), axis=0)
        out_ref[...] = part if i == 0 else out_ref[...] + part


def total_of(got):
    _, rows, width = got.shape
    return pl.pallas_call(
        total_kernel,
        in_specs=[pl.BlockSpec(memory_space=pltpu.HBM)],
        out_specs=VMEM,
        scratch_shapes=[pltpu.VMEM((4, 4, rows, width), BF16), pltpu.SemaphoreType.DMA((4,))],
        out_shape=jax.ShapeDtypeStruct((rows, width), F32),
        compiler_params=pltpu.CompilerParams(vmem_limit_bytes=LIMIT),
        name="total",
    )(got)


def sums_kernel(at, near_ref, near_in_ref, far_ref, far_in_ref, out_ref):
    zlo = at[2]
    for kx in range(2):
        for ky in range(2):
            out_ref[zlo, kx, ky] = (near_ref[kx, 0, ky] + near_in_ref[kx, ky].astype(F32)).astype(BF16)
            out_ref[1 - zlo, kx, ky] = (far_ref[kx, ky, 0] + far_in_ref[kx, ky].astype(F32)).astype(BF16)


def sums(at, near, near_in, far, far_in):
    out = (2, *near_in.shape)
    return pl.pallas_call(
        sums_kernel,
        in_specs=[SCALAR] + [VMEM] * 4,
        out_specs=VMEM,
        out_shape=jax.ShapeDtypeStruct(out, BF16),
        compiler_params=pltpu.CompilerParams(vmem_limit_bytes=LIMIT),
        name="sums",
    )(at, near, near_in, far, far_in)


def local(tokens, positions, weight_codes, weight_scales, key_cotangent):
    x, y, zlo, zhi, core = coordinates(lax.axis_index(BITS))
    at = jnp.stack([x, y, zlo, zhi, core]).astype(jnp.int32)
    tie = lax.optimization_barrier

    weight = weight_piece(at, weight_codes, weight_scales.T)
    weight_got = send("weight_y_near", weight, y=NEAR)

    freq = 10000.0 ** (-(2.0 * jnp.arange(HALF, dtype=F32)) / HD)
    angle = freq[:, None] * positions.astype(F32)[None, :]
    cos, sin = jnp.cos(angle), jnp.sin(angle)
    back = back_of(key_cotangent, cos, sin)

    far, far_sib = grad_half(at, back, tokens, 1)
    far, far_sib, back, weight, weight_got = tie((far, far_sib, back, weight, weight_got))
    far_got = send("far_core", far_sib, core=(1, 1))
    weight = jnp.concatenate([weight, weight_got])
    back, weight = tie((back, weight))
    weight_got = send("weight_y_back", weight, y=BACK)
    part_got = send("weight_z_near", weight, z=NEAR)
    near, near_sib = grad_half(at, back, tokens, 0)
    near, near_sib, far_got, weight_got, part_got = tie((near, near_sib, far_got, weight_got, part_got))
    near_got = send("near_core", near_sib, core=(1, 1))
    parts = [jnp.concatenate([weight, part_got])]
    part_got = send("weight_z_near_late", weight_got, z=NEAR)
    late = [send("weight_z_back", parts[0], z=BACK)]
    sib = [send("weight_core_0", parts[0], core=(1, 1))]

    def total(own, got, ax, ay):
        return own[:, ax, :, ay] + got[:, ax, :, ay].astype(F32)

    both = slice(None)
    far_in = send("far_x", total(far, far_got, 1, both).astype(BF16), x=NEAR)
    near_in = send("near_y", total(near, near_got, both, 1).astype(BF16), y=NEAR)
    far_sent = (total(far, far_got, 0, 1) + far_in[:, :, 1].astype(F32)).astype(BF16)
    near_sent = (total(near, near_got, 1, 0) + near_in[:, 1].astype(F32)).astype(BF16)
    far = total(far, far_got, 0, both) + far_in.astype(F32)
    near = total(near, near_got, both, 0) + near_in.astype(F32)
    far_in = send("far_y", far_sent, y=NEAR)
    near_in = send("near_x", near_sent, x=NEAR)
    part_got, _, _ = tie((part_got, far_sent, near_sent))
    parts.append(jnp.concatenate([weight_got, part_got]))
    late.append(send("weight_z_back_late", parts[1], z=BACK))
    sib += [send("weight_core_1", parts[1], core=(1, 1)), send("weight_core_2", late[0], core=(1, 1))]
    mine = sums(at, near, near_in, far, far_in).reshape(16, 64, 512)
    got = lax.all_to_all(mine, BITS, 0, 0, axis_index_groups=quads(), tiled=True)
    at, late[1], _ = tie((at, late[1], mine))
    sib.append(send("weight_core_3", late[1], core=(1, 1)))
    half = forward(at, tokens, parts + late)
    keys = forward(at, tokens, sib, half, cos, sin)
    keys, got = tie((keys, got))
    return keys, total_of(got)


def solution(mesh):
    bits = Mesh(mesh.devices.reshape((2,) * 7), BITS)
    tokens, weight = P(BITS, None), P(("yhi", "ylo", "zhi", "core"), None)
    return jax.shard_map(
        local,
        mesh=bits,
        in_specs=(tokens, P(BITS), weight, weight, tokens),
        out_specs=(tokens, tokens),
        check_vma=False,
    )
```

```python
import jax
import jax.numpy as jnp
from jax import lax
from jax.experimental import pallas as pl
from jax.experimental.pallas import tpu as pltpu
from jax.sharding import Mesh, PartitionSpec as P

HD = 128
HALF = 64
BLOCK = 256
BF16 = jnp.bfloat16
F32 = jnp.float32
MIB = 1024 * 1024
BITS = ("zlo", "xhi", "xlo", "yhi", "ylo", "zhi", "core")
LIMIT = 8 * MIB
LARGE = 36 * MIB
VMEM = pl.BlockSpec(memory_space=pltpu.VMEM)
SCALAR = pl.BlockSpec(memory_space=pltpu.SMEM)
NEAR, BACK = (1, 3), (3, 1)


def coordinates(device):
    return (device >> 4) & 3, (device >> 2) & 3, device >> 6, (device >> 1) & 1, device & 1


def side(v, core):
    return v & 1 if core else v >> 1


def quads():
    groups = {}
    for device in range(128):
        x, y, zlo, zhi, core = coordinates(device)
        sides = side(x, core), side(y, core)
        name = core, *(v ^ BACK[core] * s for v, s in zip((x, y), sides))
        groups.setdefault(name, []).append((zlo, *sides, zhi, device))
    return [[member[-1] for member in sorted(members)] for members in groups.values()]


STAY = (0, 0)


def send(what, value, x=STAY, y=STAY, z=STAY, core=STAY):
    pairs = []
    for src in range(128):
        at_x, at_y, zlo, zhi, at_core = coordinates(src)
        at_z = (2 * zhi + zlo) ^ z[at_core]
        place = ((at_z & 1) << 6) | ((at_x ^ x[at_core]) << 4) | ((at_y ^ y[at_core]) << 2) | ((at_z >> 1) << 1)
        pairs.append((src, place | (at_core ^ core[at_core])))
    with jax.named_scope(what):
        return lax.ppermute(value, BITS, pairs)


def held_from(place, core):
    return jnp.where(core == 0, *(((0, 0), (1, 3), (3, 1), (2, 2))[place]))


def weight_kernel(at, codes_ref, scales_ref, piece_ref, scaled):
    scales = jnp.concatenate([scales_ref[...]] * 4, axis=0).T
    for block in range(2):
        columns = slice(block * BLOCK, (block + 1) * BLOCK)
        scaled[:, columns] = (codes_ref[:, columns].astype(F32) * scales[:, block : block + 1]).astype(BF16)
    piece_ref[0] = scaled[pl.ds(pl.multiple_of(at[2] * 256, 256), 256)]


def weight_piece(at, codes, scales):
    rows, width = codes.shape
    return pl.pallas_call(
        weight_kernel,
        in_specs=[SCALAR, VMEM, VMEM],
        out_specs=VMEM,
        out_shape=jax.ShapeDtypeStruct((1, rows // 2, width), BF16),
        scratch_shapes=[pltpu.VMEM((rows, width), BF16)],
        compiler_params=pltpu.CompilerParams(vmem_limit_bytes=LIMIT),
        name="weight",
    )(at, codes, scales)


def head_turn(cos_ref, sin_ref):
    cos, sin = cos_ref[...], sin_ref[...]
    return jnp.concatenate([cos, cos], axis=0).T, jnp.concatenate([-sin, sin], axis=0).T


def back_kernel(cotangent_ref, cos_ref, sin_ref, back_ref):
    cos, sin = head_turn(cos_ref, sin_ref)
    for head in range(4):
        given = cotangent_ref[:, head * HD : (head + 1) * HD].astype(F32)
        back_ref[:, head * HD : (head + 1) * HD] = (given * cos - pltpu.roll(given, HALF, 1) * sin).astype(BF16)


def back_of(cotangent, cos, sin):
    return pl.pallas_call(
        back_kernel,
        in_specs=[VMEM] * 3,
        out_specs=VMEM,
        out_shape=jax.ShapeDtypeStruct(cotangent.shape, BF16),
        compiler_params=pltpu.CompilerParams(vmem_limit_bytes=LIMIT),
        name="back",
    )(cotangent, cos, sin)


def grad_kernel(chunk, at, back_ref, tokens_ref, own_ref, sib_ref, kept_ref, arrived):
    x, y, zlo, core = at[0], at[1], at[2], at[4]

    def fetch(i):
        column = pl.multiple_of(((zlo ^ chunk) * 4 + i) * 1024, 1024)
        return pltpu.make_async_copy(tokens_ref.at[:, pl.ds(column, 1024)], kept_ref.at[i], arrived.at[i])

    def place(to, here, holder):
        low, high = (to ^ here) & 1, (to ^ here) >> 1
        return jnp.where(holder == 0, to >> 1, to & 1), high ^ (low & (1 - holder))

    for i in range(4):
        fetch(i).start()
    for i in range(4):
        fetch(i).wait()
        for pair in range(2):
            block = kept_ref[i, :, pair * 512 : (pair + 1) * 512]
            part = lax.dot_general(block, back_ref[...], (((0,), (0,)), ((), ())), preferred_element_type=F32)
            for j in range(4):
                to_y, to_zhi = 2 * pair + j // 2, j % 2
                halves = part[j * 128 : j * 128 + 64], part[j * 128 + 64 : (j + 1) * 128]
                for ref, holder, half in (
                    (own_ref, core, jnp.where(core == 0, halves[0], halves[1])),
                    (sib_ref, 1 - core, jnp.where(core == 0, halves[1], halves[0])),
                ):
                    ref[(*place(i, x, holder), *place(to_y, y, holder), to_zhi)] = half.astype(ref.dtype)


def grad_half(at, back, tokens, chunk):
    rows, width = back.shape
    blocks = (2, 2, 2, 2, 2, 64, width)
    return pl.pallas_call(
        lambda *refs: grad_kernel(chunk, *refs),
        in_specs=[SCALAR, VMEM, pl.BlockSpec(memory_space=pltpu.HBM)],
        out_specs=[VMEM, VMEM],
        out_shape=[
            jax.ShapeDtypeStruct(blocks, F32),
            jax.ShapeDtypeStruct(blocks, BF16),
        ],
        scratch_shapes=[pltpu.VMEM((4, rows, 1024), BF16), pltpu.SemaphoreType.DMA((4,))],
        compiler_params=pltpu.CompilerParams(vmem_limit_bytes=LARGE),
        cost_estimate=pl.CostEstimate(flops=20 * rows * 4096 * width, bytes_accessed=8 * MIB, transcendentals=0),
        name="grad",
    )(at, back, tokens)


def forward_kernel(parts, count, at, tokens_ref, *rest):
    y, zlo, zhi, core = at[1], at[2], at[3], at[4]
    weights, rest = rest[:count], rest[count:]
    block, arrived = rest[-2:]

    def fetch(n, quarter):
        z_half, y_half, other, _, _ = parts[n]
        holder = core ^ other
        to_y = y ^ held_from(2 * y_half + quarter % 2, holder)
        to_z = (2 * zhi + zlo) ^ held_from(2 * z_half + quarter // 2, holder)
        column = ((to_y * 2 + to_z // 2) * 2 + holder) * 512 + (to_z % 2) * 256
        return pltpu.make_async_copy(
            tokens_ref.at[:, pl.ds(pl.multiple_of(column, 256), 256)],
            block.at[n, :, quarter * 256 : (quarter + 1) * 256],
            arrived.at[n, quarter],
        )

    for n in range(len(parts)):
        for quarter in range(4):
            fetch(n, quarter).start()
    total = rest[0] if len(rest) > 3 else None
    out = rest[-3]
    for n, (_, _, _, place, start) in enumerate(parts):
        for quarter in range(4):
            fetch(n, quarter).wait()
        weight = weights[place][start : start + 4].reshape(1024, 512)
        product = jnp.dot(block[n], weight, preferred_element_type=F32)
        out[...] = product if total is None else total[...] + product
        total = out
    if len(rest) > 4:
        cos, sin = head_turn(*rest[1:3])
        keys_ref = rest[3]
        for head in range(4):
            raw = out[:, head * HD : (head + 1) * HD]
            turned = pltpu.roll(raw, HALF, 1)
            keys_ref[:, head * HD : (head + 1) * HD] = (raw * cos + turned * sin).astype(BF16)


def forward(at, tokens, parts, weights, *rest, cover=1):
    rows, _ = tokens.shape
    width = weights[0].shape[-1]
    last = len(rest) == 3
    total = pltpu.VMEM((rows, width), F32)
    return pl.pallas_call(
        lambda *refs: forward_kernel(parts, len(weights), *refs),
        in_specs=[SCALAR, pl.BlockSpec(memory_space=pltpu.HBM)] + [VMEM] * (len(weights) + len(rest)),
        out_specs=VMEM,
        scratch_shapes=[total] * last
        + [pltpu.VMEM((len(parts), rows, 1024), BF16), pltpu.SemaphoreType.DMA((len(parts), 4))],
        out_shape=jax.ShapeDtypeStruct((rows, width), BF16 if last else F32),
        compiler_params=pltpu.CompilerParams(vmem_limit_bytes=LARGE),
        cost_estimate=pl.CostEstimate(flops=cover * rows * 1024 * width, bytes_accessed=MIB, transcendentals=0),
        name="forward",
    )(at, tokens, *weights, *rest)


def total_kernel(got_ref, out_ref, block, arrived):
    def fetch(i):
        return pltpu.make_async_copy(got_ref.at[4 * i : 4 * i + 4], block.at[i], arrived.at[i])

    for i in range(4):
        fetch(i).start()
    for i in range(4):
        fetch(i).wait()
        part = jnp.sum(block[i].astype(F32), axis=0)
        out_ref[...] = part if i == 0 else out_ref[...] + part


def total_of(got):
    _, rows, width = got.shape
    return pl.pallas_call(
        total_kernel,
        in_specs=[pl.BlockSpec(memory_space=pltpu.HBM)],
        out_specs=VMEM,
        scratch_shapes=[pltpu.VMEM((4, 4, rows, width), BF16), pltpu.SemaphoreType.DMA((4,))],
        out_shape=jax.ShapeDtypeStruct((rows, width), F32),
        compiler_params=pltpu.CompilerParams(vmem_limit_bytes=LIMIT),
        name="total",
    )(got)


def sums_kernel(at, near_ref, near_in_ref, far_ref, far_in_ref, out_ref):
    zlo = at[2]
    for kx in range(2):
        for ky in range(2):
            out_ref[zlo, kx, ky] = (near_ref[kx, 0, ky] + near_in_ref[kx, ky].astype(F32)).astype(BF16)
            out_ref[1 - zlo, kx, ky] = (far_ref[kx, ky, 0] + far_in_ref[kx, ky].astype(F32)).astype(BF16)


def sums(at, near, near_in, far, far_in):
    out = (2, *near_in.shape)
    return pl.pallas_call(
        sums_kernel,
        in_specs=[SCALAR] + [VMEM] * 4,
        out_specs=VMEM,
        out_shape=jax.ShapeDtypeStruct(out, BF16),
        compiler_params=pltpu.CompilerParams(vmem_limit_bytes=LIMIT),
        name="sums",
    )(at, near, near_in, far, far_in)


def local(tokens, positions, weight_codes, weight_scales, key_cotangent):
    x, y, zlo, zhi, core = coordinates(lax.axis_index(BITS))
    at = jnp.stack([x, y, zlo, zhi, core]).astype(jnp.int32)
    tie = lax.optimization_barrier

    weight = weight_piece(at, weight_codes, weight_scales.T)
    weight_got = send("weight_y_near", weight, y=NEAR)

    freq = 10000.0 ** (-(2.0 * jnp.arange(HALF, dtype=F32)) / HD)
    angle = freq[:, None] * positions.astype(F32)[None, :]
    cos, sin = jnp.cos(angle), jnp.sin(angle)
    back = back_of(key_cotangent, cos, sin)

    far, far_sib = grad_half(at, back, tokens, 1)
    far, far_sib, back, weight, weight_got = tie((far, far_sib, back, weight, weight_got))
    far_got = send("far_core", far_sib, core=(1, 1))
    weight = jnp.concatenate([weight, weight_got])
    back, weight = tie((back, weight))
    weight_got = send("weight_y_back", weight, y=BACK)
    part_got = send("weight_z_near", weight, z=NEAR)
    near, near_sib = grad_half(at, back, tokens, 0)
    near, near_sib, far_got, weight_got, part_got = tie((near, near_sib, far_got, weight_got, part_got))
    near_got = send("near_core", near_sib, core=(1, 1))
    parts = [jnp.concatenate([weight, part_got])]
    part_got = send("weight_z_near_late", weight_got, z=NEAR)
    late = [send("weight_z_back", parts[0], z=BACK)]
    sib = [send("weight_core_0", parts[0], core=(1, 1))]

    def total(own, got, ax, ay):
        return own[:, ax, :, ay] + got[:, ax, :, ay].astype(F32)

    both = slice(None)
    far_in = send("far_x", total(far, far_got, 1, both).astype(BF16), x=NEAR)
    near_in = send("near_y", total(near, near_got, both, 1).astype(BF16), y=NEAR)
    far_sent = (total(far, far_got, 0, 1) + far_in[:, :, 1].astype(F32)).astype(BF16)
    near_sent = (total(near, near_got, 1, 0) + near_in[:, 1].astype(F32)).astype(BF16)
    far = total(far, far_got, 0, both) + far_in.astype(F32)
    near = total(near, near_got, both, 0) + near_in.astype(F32)
    far_in = send("far_y", far_sent, y=NEAR)
    near_in = send("near_x", near_sent, x=NEAR)
    part_got, _, _ = tie((part_got, far_sent, near_sent))
    parts.append(jnp.concatenate([weight_got, part_got]))
    late.append(send("weight_z_back_late", parts[1], z=BACK))
    sib += [send("weight_core_1", parts[1], core=(1, 1))]
    at, _, _ = tie((at, far_sent, near_sent))
    half = forward(
        at, tokens, [(0, 0, 0, 0, 0), (0, 0, 1, 1, 0)], [parts[0], sib[0]], cover=24
    )
    half, far_in, near_in = tie((half, far_in, near_in))
    mine = sums(at, near, near_in, far, far_in).reshape(16, 64, 512)
    got = lax.all_to_all(mine, BITS, 0, 0, axis_index_groups=quads(), tiled=True)
    at, late[0], late[1], _ = tie((at, late[0], late[1], mine))
    sib += [send("weight_core_2", late[0], core=(1, 1)), send("weight_core_3", late[1], core=(1, 1))]
    half = forward(
        at,
        tokens,
        [(0, 1, 0, 0, 0), (1, 0, 0, 1, 0), (1, 1, 0, 2, 0), (0, 1, 1, 3, 0)],
        [parts[1], late[0], late[1], sib[1]],
        half,
        cover=32,
    )
    keys = forward(at, tokens, [(1, 0, 1, 0, 0), (1, 1, 1, 1, 0)], [sib[2], sib[3]], half, cos, sin, cover=16)
    keys, got = tie((keys, got))
    return keys, total_of(got)


def solution(mesh):
    bits = Mesh(mesh.devices.reshape((2,) * 7), BITS)
    tokens, weight = P(BITS, None), P(("yhi", "ylo", "zhi", "core"), None)
    return jax.shard_map(
        local,
        mesh=bits,
        in_specs=(tokens, P(BITS), weight, weight, tokens),
        out_specs=(tokens, tokens),
        check_vma=False,
    )
```

```python
import jax
import jax.numpy as jnp
from jax import lax
from jax.experimental import pallas as pl
from jax.experimental.pallas import tpu as pltpu
from jax.sharding import Mesh, PartitionSpec as P

HD = 128
HALF = 64
BLOCK = 256
BF16 = jnp.bfloat16
F32 = jnp.float32
MIB = 1024 * 1024
BITS = ("zlo", "xhi", "xlo", "yhi", "ylo", "zhi", "core")
LIMIT = 8 * MIB
LARGE = 36 * MIB
VMEM = pl.BlockSpec(memory_space=pltpu.VMEM)
SCALAR = pl.BlockSpec(memory_space=pltpu.SMEM)
NEAR, BACK = (1, 3), (3, 1)


def coordinates(device):
    return (device >> 4) & 3, (device >> 2) & 3, device >> 6, (device >> 1) & 1, device & 1


def side(v, core):
    return v & 1 if core else v >> 1


def quads():
    groups = {}
    for device in range(128):
        x, y, zlo, zhi, core = coordinates(device)
        sides = side(x, core), side(y, core)
        name = core, *(v ^ BACK[core] * s for v, s in zip((x, y), sides))
        groups.setdefault(name, []).append((zlo, *sides, zhi, device))
    return [[member[-1] for member in sorted(members)] for members in groups.values()]


STAY = (0, 0)


def send(what, value, x=STAY, y=STAY, z=STAY, core=STAY):
    pairs = []
    for src in range(128):
        at_x, at_y, zlo, zhi, at_core = coordinates(src)
        at_z = (2 * zhi + zlo) ^ z[at_core]
        place = ((at_z & 1) << 6) | ((at_x ^ x[at_core]) << 4) | ((at_y ^ y[at_core]) << 2) | ((at_z >> 1) << 1)
        pairs.append((src, place | (at_core ^ core[at_core])))
    with jax.named_scope(what):
        return lax.ppermute(value, BITS, pairs)


def held_from(place, core):
    return jnp.where(core == 0, *(((0, 0), (1, 3), (3, 1), (2, 2))[place]))


def weight_kernel(at, codes_ref, scales_ref, piece_ref, scaled):
    scales = jnp.concatenate([scales_ref[...]] * 4, axis=0).T
    for block in range(2):
        columns = slice(block * BLOCK, (block + 1) * BLOCK)
        scaled[:, columns] = (codes_ref[:, columns].astype(F32) * scales[:, block : block + 1]).astype(BF16)
    piece_ref[0] = scaled[pl.ds(pl.multiple_of(at[2] * 256, 256), 256)]


def weight_piece(at, codes, scales):
    rows, width = codes.shape
    return pl.pallas_call(
        weight_kernel,
        in_specs=[SCALAR, VMEM, VMEM],
        out_specs=VMEM,
        out_shape=jax.ShapeDtypeStruct((1, rows // 2, width), BF16),
        scratch_shapes=[pltpu.VMEM((rows, width), BF16)],
        compiler_params=pltpu.CompilerParams(vmem_limit_bytes=LIMIT),
        name="weight",
    )(at, codes, scales)


def head_turn(cos_ref, sin_ref):
    cos, sin = cos_ref[...], sin_ref[...]
    return jnp.concatenate([cos, cos], axis=0).T, jnp.concatenate([-sin, sin], axis=0).T


def back_kernel(cotangent_ref, cos_ref, sin_ref, back_ref):
    cos, sin = head_turn(cos_ref, sin_ref)
    for head in range(4):
        given = cotangent_ref[:, head * HD : (head + 1) * HD].astype(F32)
        back_ref[:, head * HD : (head + 1) * HD] = (given * cos - pltpu.roll(given, HALF, 1) * sin).astype(BF16)


def back_of(cotangent, cos, sin):
    return pl.pallas_call(
        back_kernel,
        in_specs=[VMEM] * 3,
        out_specs=VMEM,
        out_shape=jax.ShapeDtypeStruct(cotangent.shape, BF16),
        compiler_params=pltpu.CompilerParams(vmem_limit_bytes=LIMIT),
        name="back",
    )(cotangent, cos, sin)


def grad_kernel(chunk, at, back_ref, tokens_ref, own_ref, sib_ref, kept_ref, arrived):
    x, y, zlo, core = at[0], at[1], at[2], at[4]

    def fetch(i):
        column = pl.multiple_of(((zlo ^ chunk) * 4 + i) * 1024, 1024)
        return pltpu.make_async_copy(tokens_ref.at[:, pl.ds(column, 1024)], kept_ref.at[i], arrived.at[i])

    def place(to, here, holder):
        low, high = (to ^ here) & 1, (to ^ here) >> 1
        return jnp.where(holder == 0, to >> 1, to & 1), high ^ (low & (1 - holder))

    for i in range(4):
        fetch(i).start()
    for i in range(4):
        fetch(i).wait()
        for pair in range(2):
            block = kept_ref[i, :, pair * 512 : (pair + 1) * 512]
            part = lax.dot_general(block, back_ref[...], (((0,), (0,)), ((), ())), preferred_element_type=F32)
            for j in range(4):
                to_y, to_zhi = 2 * pair + j // 2, j % 2
                halves = part[j * 128 : j * 128 + 64], part[j * 128 + 64 : (j + 1) * 128]
                for ref, holder, half in (
                    (own_ref, core, jnp.where(core == 0, halves[0], halves[1])),
                    (sib_ref, 1 - core, jnp.where(core == 0, halves[1], halves[0])),
                ):
                    ref[(*place(i, x, holder), *place(to_y, y, holder), to_zhi)] = half.astype(ref.dtype)


def grad_half(at, back, tokens, chunk):
    rows, width = back.shape
    blocks = (2, 2, 2, 2, 2, 64, width)
    return pl.pallas_call(
        lambda *refs: grad_kernel(chunk, *refs),
        in_specs=[SCALAR, VMEM, pl.BlockSpec(memory_space=pltpu.HBM)],
        out_specs=[VMEM, VMEM],
        out_shape=[
            jax.ShapeDtypeStruct(blocks, F32),
            jax.ShapeDtypeStruct(blocks, BF16),
        ],
        scratch_shapes=[pltpu.VMEM((4, rows, 1024), BF16), pltpu.SemaphoreType.DMA((4,))],
        compiler_params=pltpu.CompilerParams(vmem_limit_bytes=LARGE),
        cost_estimate=pl.CostEstimate(flops=20 * rows * 4096 * width, bytes_accessed=8 * MIB, transcendentals=0),
        name="grad",
    )(at, back, tokens)


def forward_kernel(parts, count, at, tokens_ref, *rest):
    y, zlo, zhi, core = at[1], at[2], at[3], at[4]
    weights, rest = rest[:count], rest[count:]
    block, arrived = rest[-2:]

    def fetch(n, quarter):
        z_half, y_half, other, _, _ = parts[n]
        holder = core ^ other
        to_y = y ^ held_from(2 * y_half + quarter % 2, holder)
        to_z = (2 * zhi + zlo) ^ held_from(2 * z_half + quarter // 2, holder)
        column = ((to_y * 2 + to_z // 2) * 2 + holder) * 512 + (to_z % 2) * 256
        return pltpu.make_async_copy(
            tokens_ref.at[:, pl.ds(pl.multiple_of(column, 256), 256)],
            block.at[n, :, quarter * 256 : (quarter + 1) * 256],
            arrived.at[n, quarter],
        )

    for n in range(len(parts)):
        for quarter in range(4):
            fetch(n, quarter).start()
    total = rest[0] if len(rest) > 3 else None
    out = rest[-3]
    for n, (_, _, _, place, start) in enumerate(parts):
        for quarter in range(4):
            fetch(n, quarter).wait()
        weight = weights[place][start : start + 4].reshape(1024, 512)
        product = jnp.dot(block[n], weight, preferred_element_type=F32)
        out[...] = product if total is None else total[...] + product
        total = out
    if len(rest) > 4:
        cos, sin = head_turn(*rest[1:3])
        keys_ref = rest[3]
        for head in range(4):
            raw = out[:, head * HD : (head + 1) * HD]
            turned = pltpu.roll(raw, HALF, 1)
            keys_ref[:, head * HD : (head + 1) * HD] = (raw * cos + turned * sin).astype(BF16)


def forward(at, tokens, parts, weights, *rest, cover=1):
    rows, _ = tokens.shape
    width = weights[0].shape[-1]
    last = len(rest) == 3
    total = pltpu.VMEM((rows, width), F32)
    return pl.pallas_call(
        lambda *refs: forward_kernel(parts, len(weights), *refs),
        in_specs=[SCALAR, pl.BlockSpec(memory_space=pltpu.HBM)] + [VMEM] * (len(weights) + len(rest)),
        out_specs=VMEM,
        scratch_shapes=[total] * last
        + [pltpu.VMEM((len(parts), rows, 1024), BF16), pltpu.SemaphoreType.DMA((len(parts), 4))],
        out_shape=jax.ShapeDtypeStruct((rows, width), BF16 if last else F32),
        compiler_params=pltpu.CompilerParams(vmem_limit_bytes=LARGE),
        cost_estimate=pl.CostEstimate(flops=cover * rows * 1024 * width, bytes_accessed=MIB, transcendentals=0),
        name="forward",
    )(at, tokens, *weights, *rest)


def total_kernel(got_ref, out_ref, block, arrived):
    def fetch(i):
        return pltpu.make_async_copy(got_ref.at[4 * i : 4 * i + 4], block.at[i], arrived.at[i])

    for i in range(4):
        fetch(i).start()
    for i in range(4):
        fetch(i).wait()
        part = jnp.sum(block[i].astype(F32), axis=0)
        out_ref[...] = part if i == 0 else out_ref[...] + part


def total_of(got):
    _, rows, width = got.shape
    return pl.pallas_call(
        total_kernel,
        in_specs=[pl.BlockSpec(memory_space=pltpu.HBM)],
        out_specs=VMEM,
        scratch_shapes=[pltpu.VMEM((4, 4, rows, width), BF16), pltpu.SemaphoreType.DMA((4,))],
        out_shape=jax.ShapeDtypeStruct((rows, width), F32),
        compiler_params=pltpu.CompilerParams(vmem_limit_bytes=LIMIT),
        name="total",
    )(got)


def sums_kernel(at, near_ref, near_in_ref, far_ref, far_in_ref, out_ref):
    zlo = at[2]
    for kx in range(2):
        for ky in range(2):
            out_ref[zlo, kx, ky] = (near_ref[kx, 0, ky] + near_in_ref[kx, ky].astype(F32)).astype(BF16)
            out_ref[1 - zlo, kx, ky] = (far_ref[kx, ky, 0] + far_in_ref[kx, ky].astype(F32)).astype(BF16)


def sums(at, near, near_in, far, far_in):
    out = (2, *near_in.shape)
    return pl.pallas_call(
        sums_kernel,
        in_specs=[SCALAR] + [VMEM] * 4,
        out_specs=VMEM,
        out_shape=jax.ShapeDtypeStruct(out, BF16),
        compiler_params=pltpu.CompilerParams(vmem_limit_bytes=LIMIT),
        name="sums",
    )(at, near, near_in, far, far_in)


def local(tokens, positions, weight_codes, weight_scales, key_cotangent):
    x, y, zlo, zhi, core = coordinates(lax.axis_index(BITS))
    at = jnp.stack([x, y, zlo, zhi, core]).astype(jnp.int32)
    tie = lax.optimization_barrier

    weight = weight_piece(at, weight_codes, weight_scales.T)
    weight_got = send("weight_y_near", weight, y=NEAR)

    freq = 10000.0 ** (-(2.0 * jnp.arange(HALF, dtype=F32)) / HD)
    angle = freq[:, None] * positions.astype(F32)[None, :]
    cos, sin = jnp.cos(angle), jnp.sin(angle)
    back = back_of(key_cotangent, cos, sin)

    far, far_sib = grad_half(at, back, tokens, 1)
    far, far_sib, back, weight, weight_got = tie((far, far_sib, back, weight, weight_got))
    far_got = send("far_core", far_sib, core=(1, 1))
    weight = jnp.concatenate([weight, weight_got])
    back, weight = tie((back, weight))
    weight_got = send("weight_y_back", weight, y=BACK)
    part_got = send("weight_z_near", weight, z=NEAR)
    near, near_sib = grad_half(at, back, tokens, 0)
    near, near_sib, far_got, weight_got, part_got = tie((near, near_sib, far_got, weight_got, part_got))
    near_got = send("near_core", near_sib, core=(1, 1))
    parts = [jnp.concatenate([weight, part_got])]
    part_got = send("weight_z_near_late", weight_got, z=NEAR)
    late = [send("weight_z_back", parts[0], z=BACK)]
    sib = [send("weight_core_0", parts[0], core=(1, 1))]

    def total(own, got, ax, ay):
        return own[:, ax, :, ay] + got[:, ax, :, ay].astype(F32)

    both = slice(None)
    far_in = send("far_x", total(far, far_got, 1, both).astype(BF16), x=NEAR)
    near_in = send("near_y", total(near, near_got, both, 1).astype(BF16), y=NEAR)
    far_sent = (total(far, far_got, 0, 1) + far_in[:, :, 1].astype(F32)).astype(BF16)
    near_sent = (total(near, near_got, 1, 0) + near_in[:, 1].astype(F32)).astype(BF16)
    far = total(far, far_got, 0, both) + far_in.astype(F32)
    near = total(near, near_got, both, 0) + near_in.astype(F32)
    far_in = send("far_y", far_sent, y=NEAR)
    near_in = send("near_x", near_sent, x=NEAR)
    part_got, _, _ = tie((part_got, far_sent, near_sent))
    parts.append(jnp.concatenate([weight_got, part_got]))
    late.append(send("weight_z_back_late", parts[1], z=BACK))
    sib += [send("weight_core_1", parts[1], core=(1, 1))]
    at, _, _ = tie((at, far_sent, near_sent))
    half = forward(
        at, tokens, [(0, 0, 0, 0, 0)], [parts[0]], cover=24
    )
    half, far_in, near_in = tie((half, far_in, near_in))
    mine = sums(at, near, near_in, far, far_in).reshape(16, 64, 512)
    got = lax.all_to_all(mine, BITS, 0, 0, axis_index_groups=quads(), tiled=True)
    at, late[0], late[1], _ = tie((at, late[0], late[1], mine))
    sib += [send("weight_core_2", late[0], core=(1, 1)), send("weight_core_3", late[1], core=(1, 1))]
    half = forward(
        at,
        tokens,
        [(0, 1, 0, 0, 0), (1, 0, 0, 1, 0), (1, 1, 0, 2, 0), (0, 0, 1, 4, 0), (0, 1, 1, 3, 0)],
        [parts[1], late[0], late[1], sib[1], sib[0]],
        half,
        cover=32,
    )
    keys = forward(at, tokens, [(1, 0, 1, 0, 0), (1, 1, 1, 1, 0)], [sib[2], sib[3]], half, cos, sin, cover=16)
    keys, got = tie((keys, got))
    return keys, total_of(got)


def solution(mesh):
    bits = Mesh(mesh.devices.reshape((2,) * 7), BITS)
    tokens, weight = P(BITS, None), P(("yhi", "ylo", "zhi", "core"), None)
    return jax.shard_map(
        local,
        mesh=bits,
        in_specs=(tokens, P(BITS), weight, weight, tokens),
        out_specs=(tokens, tokens),
        check_vma=False,
    )
```
